32 devices in a mesh: layer: 8 (over z, x), shot: 4 (over y, core).
Axes of the slice: x: 2, y: 2, z: 4, core: 2. Of those that a mesh axis runs over, the one named last changes fastest.
Arguments:
- down_state: bfloat16 [8, 1024, 2048], P('layer', None, 'shot'), may hold values from -6 to 6
- up_state: bfloat16 [8, 1024, 2048], P('layer', None, 'shot'), may hold values from -6 to 6
- down_op: bfloat16 [8, 1024, 1024], P('layer', 'shot'), may hold values from -0.1875 to 0.1875
- up_op: bfloat16 [8, 1024, 1024], P('layer', 'shot'), may hold values from -0.1875 to 0.1875
- reflect_op: bfloat16 [8, 1024, 1024], P('layer', 'shot'), may hold values from -0.125 to 0.125
- source_bank: bfloat16 [8, 2, 1024, 2048], P('layer', None, None, 'shot'), may hold values from -4 to 4
- plan: int32 [4, 8], P(None, 'layer'), may hold values from 0 to 1
- layer_source: int32 [8], P('layer'), may hold values from 0 to 1
Outputs:
- down_out: bfloat16 [8, 1024, 2048], P('layer', None, 'shot')
- up_out: bfloat16 [8, 1024, 2048], P('layer', None, 'shot')
The draws below stay inside these ranges and needn't reach their ends.
All inputs are finite; a program needn't handle non-finite values.
Results may differ from the reference program's by a relative error of at most 0.008.
Values may be sent and summed in bfloat16 or wider, within the bound.
A program may use at most 64 MiB of HBM per device.

```python
import jax
import jax.numpy as jnp
from jax import lax

M = 1024
NSRC = 2
TICKS = 4
LAYERS = 8
SHOTS = 2048


def touch_ends(result, own_key, smallest, high):
    shape = result.shape
    spot = [jax.random.randint(jax.random.fold_in(own_key, axis), (), 0, shape[axis]) for axis in range(len(shape))]
    result = result.at[tuple(spot)].set(smallest)
    longest = shape.index(max(shape))
    spot[longest] = (spot[longest] + 1) % shape[longest]
    return result.at[tuple(spot)].set(high)


def block_scale(rng, dims, pieces, least, largest):
    def one(axis_at, parts):
        steps = jax.random.uniform(jax.random.fold_in(jax.random.fold_in(rng, 6), axis_at), (parts,), jnp.float32, least / len(pieces), largest / len(pieces))
        return jnp.repeat(jnp.exp(steps), dims[axis_at] // parts).reshape((-1,) + (1,) * (len(dims) - axis_at - 1))

    loudness = one(*pieces[0])
    for cut in pieces[1:]:
        loudness = loudness * one(*cut)
    return loudness


def normal_values(key, extent, width, most, split=(), kind=jnp.bfloat16):
    result = width * jax.random.normal(key, extent, jnp.float32)
    if split:
        result = result * block_scale(key, extent, split, -0.22, 0.18)
    return jnp.clip(result, -most, most).astype(kind)


def setup_inputs(seed: int = 0) -> dict:
    key_of = jax.random.split(jax.random.key(seed), 9)
    return {
        "down_state": normal_values(key_of[0], (LAYERS, M, SHOTS), 1.0, 6.0, ((0, 8), (2, 4))),
        "up_state": normal_values(key_of[1], (LAYERS, M, SHOTS), 1.0, 6.0, ((0, 8), (2, 4))),
        "down_op": normal_values(key_of[2], (LAYERS, M, M), M ** -0.5, 0.1875, ((0, 8), (1, 4))),
        "up_op": normal_values(key_of[3], (LAYERS, M, M), M ** -0.5, 0.1875, ((0, 8), (1, 4))),
        "reflect_op": normal_values(key_of[4], (LAYERS, M, M), (2 * M) ** -0.5, 0.125, ((0, 8), (1, 4))),
        "source_bank": normal_values(key_of[5], (LAYERS, NSRC, M, SHOTS), 0.5, 4.0, ((0, 8), (3, 4))),
        "plan": touch_ends(jax.random.randint(key_of[6], (TICKS, LAYERS), 0, NSRC), jax.random.fold_in(key_of[6], 1), 0, NSRC - 1).astype(jnp.int32),
        "layer_source": touch_ends(jax.random.randint(key_of[7], (LAYERS,), 0, NSRC), jax.random.fold_in(key_of[7], 1), 0, NSRC - 1).astype(jnp.int32),
    }


def layer_update(operands):
    down_block, up_block, reflect_block, down_in, received_up, upward_source = operands
    new_down = jnp.dot(down_block, down_in, preferred_element_type=jnp.float32).astype(jnp.bfloat16)
    total = jnp.dot(up_block, received_up, preferred_element_type=jnp.float32)
    total = total + jnp.dot(reflect_block, down_in, preferred_element_type=jnp.float32)
    total = total + upward_source.astype(jnp.float32)
    return new_down, total.astype(jnp.bfloat16)


def reference(down_state, up_state, down_op, up_op, reflect_op, source_bank, plan, layer_source):
    layer_ids = jnp.arange(LAYERS, dtype=jnp.int32)
    downgoing = down_state
    upgoing = up_state
    upward_source = source_bank[layer_ids, layer_source.astype(jnp.int32)]
    for moment in range(TICKS):
        received_down = jnp.concatenate([jnp.zeros_like(downgoing[:1]), downgoing[:-1]], axis=0)
        received_up = jnp.concatenate([upgoing[1:], jnp.zeros_like(upgoing[:1])], axis=0)
        injected = source_bank[layer_ids, plan[moment].astype(jnp.int32)]
        down_in = (received_down.astype(jnp.float32) + injected.astype(jnp.float32)).astype(jnp.bfloat16)
        downgoing, upgoing = lax.map(layer_update, (down_op, up_op, reflect_op, down_in, received_up, upward_source))
    return downgoing, upgoing
```

```python
import functools

import jax
import jax.numpy as jnp
from jax import lax
from jax.experimental import pallas as pl
from jax.experimental.pallas import tpu as pltpu
from jax.sharding import PartitionSpec as P

MESH = pl.DeviceIdType.MESH
LAG = 2


def low_bit(mask):
    return mask & -mask


def kernel(
    layers, shots, ticks, batches, chunks, width, tile,
    down_ref, up_ref, dop_ref, uop_ref, rop_ref, bank_ref, ctrl_ref,
    down_out, up_out,
    ops, inbuf, outbuf, bank, ctrl, mixed,
    xs, xr, cs, cr, ss, sr, gs, gr, zs, zr, lo, lt, lb, ls,
):
    me = lax.axis_index("layer")
    shot = lax.axis_index("shot")
    side = lax.rem(me, 2)
    mate = me + 1 - 2 * side
    order, block = ops.shape[2], dop_ref.shape[1]
    op_refs = (dop_ref, uop_ref, rop_ref)
    bits = [1 << i for i in reversed(range((shots - 1).bit_length()))]
    above, below = me + 2 < layers, me - 2 >= 0

    def rows(mask):
        return pl.ds(pl.multiple_of((shot ^ mask) * block, block), block)

    def cols(c):
        return pl.ds(pl.multiple_of(c * width, width), width)

    barrier = pltpu.get_barrier_semaphore()
    pl.semaphore_signal(barrier, inc=1, device_id=(mate, shot), device_id_type=MESH)
    for bit in bits:
        pl.semaphore_signal(barrier, inc=1, device_id=(me, shot ^ bit), device_id_type=MESH)

    @pl.when(above)
    def _():
        pl.semaphore_signal(barrier, inc=1, device_id=(me + 2, shot), device_id_type=MESH)

    @pl.when(below)
    def _():
        pl.semaphore_signal(barrier, inc=1, device_id=(me - 2, shot), device_id_type=MESH)

    local = []
    for k in range(3):
        local.append(pltpu.make_async_copy(op_refs[k].at[0], ops.at[0, k, rows(0)], lo.at[k]))
    for b in range(batches):
        for c in range(chunks):
            local.append(
                pltpu.make_async_copy(
                    bank_ref.at[0, b, :, pl.ds(c * width, width)], bank.at[0, b, c], lb.at[b, c]
                )
            )
    for copy in local:
        copy.start()

    def keep(c, which):
        source = up_ref if which else down_ref
        return pltpu.make_async_copy(source.at[0, :, cols(c)], inbuf.at[0, which, c], lt.at[c])

    for c in range(chunks):
        for which in (0, 1):
            pl.when(side == which)(keep(c, which).start)

    pl.semaphore_wait(barrier, 1 + len(bits) + above.astype(jnp.int32) + below.astype(jnp.int32))

    def cross(k):
        return pltpu.make_async_remote_copy(
            op_refs[k].at[0], ops.at[1, k, rows(0)], xs.at[k], xr.at[k],
            device_id=(mate, shot), device_id_type=MESH,
        )

    def spread(j, k, mask, bit):
        sem = (j, k, mask | bit)
        return pltpu.make_async_remote_copy(
            ops.at[j, k, rows(mask)], ops.at[j, k, rows(mask)], gs.at[sem], gr.at[sem],
            device_id=(me, shot ^ bit), device_id_type=MESH,
        )

    def arrived(j, k, mask):
        pltpu.make_async_copy(ops.at[j, k, rows(mask)], ops.at[j, k, rows(mask)], gr.at[j, k, mask]).wait()

    def onward(mask):
        return [bit for bit in bits if mask == 0 or bit < low_bit(mask)]

    relayed = [mask for mask in range(1, shots) if onward(mask)]
    relayed.sort(key=lambda mask: -low_bit(mask))
    settled = [mask for mask in range(1, shots) if not onward(mask)]

    def sources(b, c):
        return pltpu.make_async_remote_copy(
            bank_ref.at[0, b, :, cols(c)], bank.at[1, b, c], ss.at[b, c], sr.at[b, c],
            device_id=(mate, shot), device_id_type=MESH,
        )

    def first_to(which, c):
        source = up_ref if which else down_ref
        return pltpu.make_async_remote_copy(
            source.at[0, :, cols(c)], inbuf.at[0, which, c], zs.at[0, c], zr.at[0, c],
            device_id=(me + 2 - 4 * which, shot), device_id_type=MESH,
        )

    def pass_on(t, which, c):
        return pltpu.make_async_remote_copy(
            outbuf.at[t, c], inbuf.at[t + 1, which, c], zs.at[t + 1, c], zr.at[t + 1, c],
            device_id=(me + 2 - 4 * which, shot), device_id_type=MESH,
        )

    own_ctrl = pltpu.make_async_remote_copy(
        ctrl_ref, ctrl, cs, cr, device_id=(mate, shot), device_id_type=MESH
    )
    own_ctrl.start()
    for k in range(3):
        cross(k).start()
    for c in range(chunks):
        pl.when((side == 1) & above)(first_to(0, c).start)
        pl.when((side == 0) & below)(first_to(1, c).start)
    for k in range(3):
        local[k].wait()
        for bit in bits:
            if k == 0 or bit != bits[0]:
                spread(0, k, 0, bit).start()
    for k in range(3):
        cross(k).wait_recv()
        for bit in bits:
            spread(1, k, 0, bit).start()
    for b in range(batches):
        sources(b, 0).start()
    for mask in relayed:
        for k in range(3):
            arrived(1, k, mask)
            for bit in onward(mask):
                spread(1, k, mask, bit).start()
    for k in range(1, 3):
        spread(0, k, 0, bits[0]).start()
    for copy in local[3:]:
        copy.wait()
    for c in range(chunks):
        for which in (0, 1):
            pl.when(side == which)(keep(c, which).wait)
    own_ctrl.wait()
    for k in range(3):
        for mask in settled:
            arrived(1, k, mask)

    def picked(chosen, j, c, at):
        value = bank[j, 0, c, at, :].astype(jnp.float32)
        for b in range(1, batches):
            value = jnp.where(chosen == b, bank[j, b, c, at, :].astype(jnp.float32), value)
        return value

    def tick(t, c):
        even = lax.rem(t + side, 2) == 1
        j = 1 - lax.rem(t, 2)
        away = j == 1
        wanted = lambda row: jnp.where(away, ctrl[pl.ds(row, 1), :], ctrl_ref[pl.ds(row, 1), :])

        @pl.when(t == 0)
        def _():
            for b in range(batches):
                sources(b, c).wait_recv()

            @pl.when(c + 1 < chunks)
            def _():
                for b in range(batches):
                    sources(b, c + 1).start()

        @pl.when((t == 1) & (c == 0))
        def _():
            for mask in relayed:
                for k in range(3):
                    arrived(0, k, mask)
                    for bit in onward(mask):
                        spread(0, k, mask, bit).start()
            for k in range(3):
                for mask in settled:
                    arrived(0, k, mask)

        def mix():
            chosen = wanted(t)

            @pl.loop(0, order // tile)
            def _(r):
                at = pl.ds(pl.multiple_of(r * tile, tile), tile)
                value = inbuf[t, 0, c, at, :].astype(jnp.float32) + picked(chosen, j, c, at)
                mixed[at, :] = value.astype(mixed.dtype)

        def new_down(into):
            @pl.loop(0, order // tile)
            def _(r):
                at = pl.ds(pl.multiple_of(r * tile, tile), tile)
                total = jnp.dot(ops[j, 0, at, :], mixed[...], preferred_element_type=jnp.float32)
                into[at, :] = total.astype(into.dtype)

        def new_up(into):
            chosen = wanted(ticks)

            @pl.loop(0, order // tile)
            def _(r):
                at = pl.ds(pl.multiple_of(r * tile, tile), tile)
                total = jnp.dot(ops[j, 1, at, :], inbuf[t, 1, c], preferred_element_type=jnp.float32)
                total += jnp.dot(ops[j, 2, at, :], mixed[...], preferred_element_type=jnp.float32)
                total += picked(chosen, j, c, at)
                into[at, :] = total.astype(into.dtype)

        def received(which, there):
            @pl.when(there)
            def _():
                pltpu.make_async_copy(inbuf.at[t, which, c], inbuf.at[t, which, c], zr.at[t, c]).wait()

            @pl.when(jnp.logical_not(there))
            def _():
                inbuf[t, which, c] = jnp.zeros(inbuf.shape[3:], inbuf.dtype)

        more = t + 1 < ticks

        @pl.when(jnp.logical_not(even))
        def _():
            mix()
            new_down(outbuf.at[t, c])
            pl.when(more & above)(lambda: pass_on(t, 0, c).start())
            received(1, above)
            new_up(inbuf.at[t + 1, 1, c])

        @pl.when(even)
        def _():
            received(0, below)
            mix()
            new_up(outbuf.at[t, c])
            pl.when(more & below)(lambda: pass_on(t, 1, c).start())
            new_down(inbuf.at[t + 1, 0, c])

    @pl.loop(0, ticks + LAG * (chunks - 1))
    def _(i):
        @pl.loop(0, chunks)
        def _(c):
            t = i - LAG * c
            pl.when((t >= 0) & (t < ticks))(lambda: tick(t, c))

    last = ticks - 1
    ends_even = lax.rem(last + side, 2) == 1

    def results(kept_ref, sent_ref, which):
        made = []
        for c in range(chunks):
            at = pl.ds(c * width, width)
            made.append(pltpu.make_async_copy(inbuf.at[ticks, which, c], kept_ref.at[0, :, at], ls.at[0, c]))
            made.append(pltpu.make_async_copy(outbuf.at[last, c], sent_ref.at[0, :, at], ls.at[1, c]))
        for copy in made:
            copy.start()
        for copy in made:
            copy.wait()

    pl.when(ends_even)(lambda: results(down_out, up_out, 0))
    pl.when(jnp.logical_not(ends_even))(lambda: results(up_out, down_out, 1))

    for k in range(3):
        cross(k).wait_send()
    for j in range(2):
        for k in range(3):
            for mask in [0] + relayed:
                for bit in onward(mask):
                    spread(j, k, mask, bit).wait_send()
    for c in range(chunks):
        for b in range(batches):
            sources(b, c).wait_send()
        pl.when((side == 1) & above)(first_to(0, c).wait_send)
        pl.when((side == 0) & below)(first_to(1, c).wait_send)

    @pl.loop(0, ticks - 1)
    def _(t):
        even = lax.rem(t + side, 2) == 1
        for c in range(chunks):
            pl.when(even & below)(lambda: pass_on(t, 1, c).wait_send())
            pl.when(jnp.logical_not(even) & above)(lambda: pass_on(t, 0, c).wait_send())


def body(layers, shots, down_state, up_state, down_op, up_op, reflect_op, source_bank, plan, layer_source):
    order, columns = down_state.shape[1:]
    ticks, batches = plan.shape[0], source_bank.shape[1]
    width = 256 if columns % 256 == 0 else columns
    chunks = columns // width
    tile = 256 if order % 256 == 0 else order
    choices = jnp.concatenate([plan[:, 0], layer_source])
    depth = -(-choices.shape[0] // 8) * 8
    ctrl = jnp.broadcast_to(
        jnp.pad(choices, (0, depth - choices.shape[0]))[:, None], (depth, width)
    ).astype(jnp.int32)
    kind = down_state.dtype
    anywhere = pl.BlockSpec(memory_space=pl.ANY)
    dma = pltpu.SemaphoreType.DMA
    return pl.pallas_call(
        functools.partial(kernel, layers, shots, ticks, batches, chunks, width, tile),
        out_shape=(
            jax.ShapeDtypeStruct(down_state.shape, kind),
            jax.ShapeDtypeStruct(up_state.shape, kind),
        ),
        in_specs=[anywhere] * 6 + [pl.BlockSpec(memory_space=pltpu.VMEM)],
        out_specs=(anywhere, anywhere),
        scratch_shapes=[
            pltpu.VMEM((2, 3, order, order), kind),
            pltpu.VMEM((ticks + 1, 2, chunks, order, width), kind),
            pltpu.VMEM((ticks, chunks, order, width), kind),
            pltpu.VMEM((2, batches, chunks, order, width), kind),
            pltpu.VMEM((depth, width), jnp.int32),
            pltpu.VMEM((order, width), kind),
            dma((3,)), dma((3,)),
            dma, dma,
            dma((batches, chunks)), dma((batches, chunks)),
            dma((2, 3, shots)), dma((2, 3, shots)),
            dma((ticks, chunks)), dma((ticks, chunks)),
            dma((3,)), dma((chunks,)), dma((batches, chunks)), dma((2, chunks)),
        ],
        compiler_params=pltpu.CompilerParams(
            collective_id=0, has_side_effects=True, vmem_limit_bytes=56 * 1024 * 1024
        ),
        cost_estimate=pl.CostEstimate(
            flops=6 * ticks * order * order * columns,
            bytes_accessed=2 * (10 * order * columns), transcendentals=0,
        ),
    )(down_state, up_state, down_op, up_op, reflect_op, source_bank, ctrl)


def solution(mesh):
    placed = (
        P("layer", None, "shot"),
        P("layer", None, "shot"),
        P("layer", "shot", None),
        P("layer", "shot", None),
        P("layer", "shot", None),
        P("layer", None, None, "shot"),
        P(None, "layer"),
        P("layer"),
    )
    return jax.shard_map(
        functools.partial(body, mesh.shape["layer"], mesh.shape["shot"]),
        mesh=mesh,
        in_specs=placed,
        out_specs=(P("layer", None, "shot"), P("layer", None, "shot")),
        check_vma=False,
    )
```

```python
import functools

import jax
import jax.numpy as jnp
from jax import lax
from jax.experimental import pallas as pl
from jax.experimental.pallas import tpu as pltpu
from jax.sharding import PartitionSpec as P

MESH = pl.DeviceIdType.MESH
LAG = 1


def low_bit(mask):
    return mask & -mask


def kernel(
    layers, shots, ticks, batches, chunks, width, tile,
    down_ref, up_ref, dop_ref, uop_ref, rop_ref, bank_ref, ctrl_ref,
    down_out, up_out,
    ops, inbuf, outbuf, bank, ctrl, mixed,
    xs, xr, cs, cr, ss, sr, gs, gr, zs, zr, lo, lt, lb, ls,
):
    me = lax.axis_index("layer")
    shot = lax.axis_index("shot")
    side = lax.rem(me, 2)
    mate = me + 1 - 2 * side
    order, block = ops.shape[2], dop_ref.shape[1]
    op_refs = (dop_ref, uop_ref, rop_ref)
    bits = [1 << i for i in reversed(range((shots - 1).bit_length()))]
    above, below = me + 2 < layers, me - 2 >= 0

    def rows(mask):
        return pl.ds(pl.multiple_of((shot ^ mask) * block, block), block)

    def cols(c):
        return pl.ds(pl.multiple_of(c * width, width), width)

    barrier = pltpu.get_barrier_semaphore()
    pl.semaphore_signal(barrier, inc=1, device_id=(mate, shot), device_id_type=MESH)
    for bit in bits:
        pl.semaphore_signal(barrier, inc=1, device_id=(me, shot ^ bit), device_id_type=MESH)

    @pl.when(above)
    def _():
        pl.semaphore_signal(barrier, inc=1, device_id=(me + 2, shot), device_id_type=MESH)

    @pl.when(below)
    def _():
        pl.semaphore_signal(barrier, inc=1, device_id=(me - 2, shot), device_id_type=MESH)

    local = []
    for k in range(3):
        local.append(pltpu.make_async_copy(op_refs[k].at[0], ops.at[0, k, rows(0)], lo.at[k]))
    for b in range(batches):
        for c in range(chunks):
            local.append(
                pltpu.make_async_copy(
                    bank_ref.at[0, b, :, pl.ds(c * width, width)], bank.at[0, b, c], lb.at[b, c]
                )
            )
    for copy in local:
        copy.start()

    def keep(c, which):
        source = up_ref if which else down_ref
        return pltpu.make_async_copy(source.at[0, :, cols(c)], inbuf.at[0, which, c], lt.at[c])

    for c in range(chunks):
        for which in (0, 1):
            pl.when(side == which)(keep(c, which).start)

    pl.semaphore_wait(barrier, 1 + len(bits) + above.astype(jnp.int32) + below.astype(jnp.int32))

    def cross(k):
        return pltpu.make_async_remote_copy(
            op_refs[k].at[0], ops.at[1, k, rows(0)], xs.at[k], xr.at[k],
            device_id=(mate, shot), device_id_type=MESH,
        )

    def spread(j, k, mask, bit):
        sem = (j, k, mask | bit)
        return pltpu.make_async_remote_copy(
            ops.at[j, k, rows(mask)], ops.at[j, k, rows(mask)], gs.at[sem], gr.at[sem],
            device_id=(me, shot ^ bit), device_id_type=MESH,
        )

    def arrived(j, k, mask):
        pltpu.make_async_copy(ops.at[j, k, rows(mask)], ops.at[j, k, rows(mask)], gr.at[j, k, mask]).wait()

    def onward(mask):
        return [bit for bit in bits if mask == 0 or bit < low_bit(mask)]

    relayed = [mask for mask in range(1, shots) if onward(mask)]
    relayed.sort(key=lambda mask: -low_bit(mask))
    settled = [mask for mask in range(1, shots) if not onward(mask)]

    def sources(b, c):
        return pltpu.make_async_remote_copy(
            bank_ref.at[0, b, :, cols(c)], bank.at[1, b, c], ss.at[b, c], sr.at[b, c],
            device_id=(mate, shot), device_id_type=MESH,
        )

    def first_to(which, c):
        source = up_ref if which else down_ref
        return pltpu.make_async_remote_copy(
            source.at[0, :, cols(c)], inbuf.at[0, which, c], zs.at[0, c], zr.at[0, c],
            device_id=(me + 2 - 4 * which, shot), device_id_type=MESH,
        )

    def pass_on(t, which, c):
        return pltpu.make_async_remote_copy(
            outbuf.at[t, c], inbuf.at[t + 1, which, c], zs.at[t + 1, c], zr.at[t + 1, c],
            device_id=(me + 2 - 4 * which, shot), device_id_type=MESH,
        )

    own_ctrl = pltpu.make_async_remote_copy(
        ctrl_ref, ctrl, cs, cr, device_id=(mate, shot), device_id_type=MESH
    )
    own_ctrl.start()
    for k in range(3):
        cross(k).start()
    for c in range(chunks):
        pl.when((side == 1) & above)(first_to(0, c).start)
        pl.when((side == 0) & below)(first_to(1, c).start)
    for k in range(3):
        local[k].wait()
        for bit in bits:
            if k == 0 or bit != bits[0]:
                spread(0, k, 0, bit).start()
    for k in range(3):
        cross(k).wait_recv()
        for bit in bits:
            spread(1, k, 0, bit).start()
    for b in range(batches):
        sources(b, 0).start()
    for mask in relayed:
        for k in range(3):
            arrived(1, k, mask)
            for bit in onward(mask):
                spread(1, k, mask, bit).start()
    for k in range(1, 3):
        spread(0, k, 0, bits[0]).start()
    for copy in local[3:]:
        copy.wait()
    for c in range(chunks):
        for which in (0, 1):
            pl.when(side == which)(keep(c, which).wait)
    own_ctrl.wait()
    for k in range(3):
        for mask in settled:
            arrived(1, k, mask)

    def picked(chosen, j, c, at):
        value = bank[j, 0, c, at, :].astype(jnp.float32)
        for b in range(1, batches):
            value = jnp.where(chosen == b, bank[j, b, c, at, :].astype(jnp.float32), value)
        return value

    def tick(t, c):
        even = lax.rem(t + side, 2) == 1
        j = 1 - lax.rem(t, 2)
        away = j == 1
        wanted = lambda row: jnp.where(away, ctrl[pl.ds(row, 1), :], ctrl_ref[pl.ds(row, 1), :])

        @pl.when(t == 0)
        def _():
            for b in range(batches):
                sources(b, c).wait_recv()

            @pl.when(c + 1 < chunks)
            def _():
                for b in range(batches):
                    sources(b, c + 1).start()

        @pl.when((t == 1) & (c == 0))
        def _():
            for mask in relayed:
                for k in range(3):
                    arrived(0, k, mask)
                    for bit in onward(mask):
                        spread(0, k, mask, bit).start()
            for k in range(3):
                for mask in settled:
                    arrived(0, k, mask)

        def mix():
            chosen = wanted(t)

            @pl.loop(0, order // tile)
            def _(r):
                at = pl.ds(pl.multiple_of(r * tile, tile), tile)
                value = inbuf[t, 0, c, at, :].astype(jnp.float32) + picked(chosen, j, c, at)
                mixed[at, :] = value.astype(mixed.dtype)

        def new_down(into):
            @pl.loop(0, order // tile)
            def _(r):
                at = pl.ds(pl.multiple_of(r * tile, tile), tile)
                total = jnp.dot(ops[j, 0, at, :], mixed[...], preferred_element_type=jnp.float32)
                into[at, :] = total.astype(into.dtype)

        def new_up(into):
            chosen = wanted(ticks)

            @pl.loop(0, order // tile)
            def _(r):
                at = pl.ds(pl.multiple_of(r * tile, tile), tile)
                total = jnp.dot(ops[j, 1, at, :], inbuf[t, 1, c], preferred_element_type=jnp.float32)
                total += jnp.dot(ops[j, 2, at, :], mixed[...], preferred_element_type=jnp.float32)
                total += picked(chosen, j, c, at)
                into[at, :] = total.astype(into.dtype)

        def received(which, there):
            @pl.when(there)
            def _():
                pltpu.make_async_copy(inbuf.at[t, which, c], inbuf.at[t, which, c], zr.at[t, c]).wait()

            @pl.when(jnp.logical_not(there))
            def _():
                inbuf[t, which, c] = jnp.zeros(inbuf.shape[3:], inbuf.dtype)

        more = t + 1 < ticks

        @pl.when(jnp.logical_not(even))
        def _():
            mix()
            new_down(outbuf.at[t, c])
            pl.when(more & above)(lambda: pass_on(t, 0, c).start())
            received(1, above)
            new_up(inbuf.at[t + 1, 1, c])

        @pl.when(even)
        def _():
            received(0, below)
            mix()
            new_up(outbuf.at[t, c])
            pl.when(more & below)(lambda: pass_on(t, 1, c).start())
            new_down(inbuf.at[t + 1, 0, c])

    @pl.loop(0, ticks + LAG * (chunks - 1))
    def _(i):
        @pl.loop(0, chunks)
        def _(c):
            t = i - LAG * c
            pl.when((t >= 0) & (t < ticks))(lambda: tick(t, c))

    last = ticks - 1
    ends_even = lax.rem(last + side, 2) == 1

    def results(kept_ref, sent_ref, which):
        made = []
        for c in range(chunks):
            at = pl.ds(c * width, width)
            made.append(pltpu.make_async_copy(inbuf.at[ticks, which, c], kept_ref.at[0, :, at], ls.at[0, c]))
            made.append(pltpu.make_async_copy(outbuf.at[last, c], sent_ref.at[0, :, at], ls.at[1, c]))
        for copy in made:
            copy.start()
        for copy in made:
            copy.wait()

    pl.when(ends_even)(lambda: results(down_out, up_out, 0))
    pl.when(jnp.logical_not(ends_even))(lambda: results(up_out, down_out, 1))

    for k in range(3):
        cross(k).wait_send()
    for j in range(2):
        for k in range(3):
            for mask in [0] + relayed:
                for bit in onward(mask):
                    spread(j, k, mask, bit).wait_send()
    for c in range(chunks):
        for b in range(batches):
            sources(b, c).wait_send()
        pl.when((side == 1) & above)(first_to(0, c).wait_send)
        pl.when((side == 0) & below)(first_to(1, c).wait_send)

    @pl.loop(0, ticks - 1)
    def _(t):
        even = lax.rem(t + side, 2) == 1
        for c in range(chunks):
            pl.when(even & below)(lambda: pass_on(t, 1, c).wait_send())
            pl.when(jnp.logical_not(even) & above)(lambda: pass_on(t, 0, c).wait_send())


def body(layers, shots, down_state, up_state, down_op, up_op, reflect_op, source_bank, plan, layer_source):
    order, columns = down_state.shape[1:]
    ticks, batches = plan.shape[0], source_bank.shape[1]
    width = 256 if columns % 256 == 0 else columns
    chunks = columns // width
    tile = 512 if order % 512 == 0 else order
    choices = jnp.concatenate([plan[:, 0], layer_source])
    depth = -(-choices.shape[0] // 8) * 8
    ctrl = jnp.broadcast_to(
        jnp.pad(choices, (0, depth - choices.shape[0]))[:, None], (depth, width)
    ).astype(jnp.int32)
    kind = down_state.dtype
    anywhere = pl.BlockSpec(memory_space=pl.ANY)
    dma = pltpu.SemaphoreType.DMA
    return pl.pallas_call(
        functools.partial(kernel, layers, shots, ticks, batches, chunks, width, tile),
        out_shape=(
            jax.ShapeDtypeStruct(down_state.shape, kind),
            jax.ShapeDtypeStruct(up_state.shape, kind),
        ),
        in_specs=[anywhere] * 6 + [pl.BlockSpec(memory_space=pltpu.VMEM)],
        out_specs=(anywhere, anywhere),
        scratch_shapes=[
            pltpu.VMEM((2, 3, order, order), kind),
            pltpu.VMEM((ticks + 1, 2, chunks, order, width), kind),
            pltpu.VMEM((ticks, chunks, order, width), kind),
            pltpu.VMEM((2, batches, chunks, order, width), kind),
            pltpu.VMEM((depth, width), jnp.int32),
            pltpu.VMEM((order, width), kind),
            dma((3,)), dma((3,)),
            dma, dma,
            dma((batches, chunks)), dma((batches, chunks)),
            dma((2, 3, shots)), dma((2, 3, shots)),
            dma((ticks, chunks)), dma((ticks, chunks)),
            dma((3,)), dma((chunks,)), dma((batches, chunks)), dma((2, chunks)),
        ],
        compiler_params=pltpu.CompilerParams(
            collective_id=0, has_side_effects=True, vmem_limit_bytes=56 * 1024 * 1024
        ),
        cost_estimate=pl.CostEstimate(
            flops=6 * ticks * order * order * columns,
            bytes_accessed=2 * (10 * order * columns), transcendentals=0,
        ),
    )(down_state, up_state, down_op, up_op, reflect_op, source_bank, ctrl)


def solution(mesh):
    placed = (
        P("layer", None, "shot"),
        P("layer", None, "shot"),
        P("layer", "shot", None),
        P("layer", "shot", None),
        P("layer", "shot", None),
        P("layer", None, None, "shot"),
        P(None, "layer"),
        P("layer"),
    )
    return jax.shard_map(
        functools.partial(body, mesh.shape["layer"], mesh.shape["shot"]),
        mesh=mesh,
        in_specs=placed,
        out_specs=(P("layer", None, "shot"), P("layer", None, "shot")),
        check_vma=False,
    )
```
